256 devices in a mesh: dp: 64 (over y, x_lo, z), feat: 4 (over x_hi, core).
Axes of the slice: x: 4 (x_hi: 2, x_lo: 2; x = x_hi * 2 + x_lo), y: 4, z: 8, core: 2. Of those that a mesh axis runs over, the one named last changes fastest.
Arguments:
- embed_a: bfloat16 [16384, 4096], P('dp', 'feat'), may hold values from -300 to 300
- embed_b: bfloat16 [16384, 4096], P('dp', 'feat'), may hold values from -300 to 300
Outputs:
- grad_a: bfloat16 [16384, 4096], P('dp', 'feat')
- grad_b: bfloat16 [16384, 4096], P('dp', 'feat')
- loss_mean: float32 [], replicated
The draws below stay inside these ranges and needn't reach their ends.
All inputs are finite; a program needn't handle non-finite values.
Results may differ from the reference program's by a relative error of at most 0.008.
Values may be sent and summed in bfloat16 or wider, within the bound.
No kernel may reach another device: no remote copies, remote signals or barrier semaphores. Data moves between devices by JAX's collectives and lax.ppermute only.
A program may use at most 64 MiB of HBM per device.

```python
import jax
import jax.numpy as jnp
from jax import lax

EMBED = 4096
PAIRS = 16384


pick_count = 16


def shared_parts(key, factor_count, loading):
    noise_key, factor_key, group_key, sign_key, size_key, jitter_key = jax.random.split(key, 6)
    base_noise = jax.random.truncated_normal(noise_key, -4.0, 4.0, (PAIRS, EMBED), jnp.float32)
    factors = jax.random.truncated_normal(factor_key, -4.0, 4.0, (PAIRS, factor_count), jnp.float32)
    labels = jax.random.randint(group_key, (pick_count, EMBED), 0, factor_count)
    signs = jnp.where(jax.random.bernoulli(sign_key, 0.5, (pick_count, EMBED)), 1.0, -1.0)
    sizes = jax.random.uniform(size_key, (pick_count, EMBED), jnp.float32, 0.5, 1.5) * loading
    weights = signs * sizes
    place = jnp.arange(PAIRS, dtype=jnp.float32) / (PAIRS - 1)
    jitter = jax.random.uniform(jitter_key, (PAIRS, 1), jnp.float32, 0.7, 1.4)
    row_scale = 0.3 * jnp.power(10.0, 0.5 + (place - 0.5))[:, None] * jitter
    return (base_noise, factors, labels, weights, row_scale)


def common_part(factors, labels, weights):
    total = jnp.zeros((PAIRS, EMBED), jnp.float32)
    for pick in range(pick_count):
        total = total + weights[pick] * jnp.take(factors, labels[pick], axis=1)
    return total


def draw_embed_a(key, part):
    factor_count = EMBED // 16
    loading = 0.433
    base_noise, factors, labels, weights, row_scale = shared_parts(key, factor_count, loading)
    key = jax.random.fold_in(key, 11)
    weight_key, column_key, offset_key = jax.random.split(key, 3)
    mixing = jax.random.uniform(weight_key, (EMBED,), jnp.float32, 0.5, 1.5)
    column_scale = jnp.exp(jax.random.uniform(column_key, (EMBED,), jnp.float32, -0.7, 0.7))
    offsets = jax.random.uniform(offset_key, (EMBED,), jnp.float32, -1.0, 1.0)
    common = common_part(factors, labels, weights) * mixing
    value = row_scale * column_scale * (base_noise + common) + offsets * column_scale
    return jnp.clip(value, -300.0, 300.0).astype(jnp.bfloat16)


def draw_embed_b(key, part):
    factor_count = EMBED // 16
    loading = 0.433
    base_noise, factors, labels, weights, row_scale = shared_parts(key, factor_count, loading)
    key = jax.random.fold_in(key, 23)
    weight_key, column_key, offset_key, rho_key, noise_key = jax.random.split(key, 5)
    mixing = jax.random.uniform(weight_key, (EMBED,), jnp.float32, 0.5, 1.5)
    column_scale = jnp.exp(jax.random.uniform(column_key, (EMBED,), jnp.float32, -0.7, 0.7))
    offsets = jax.random.uniform(offset_key, (EMBED,), jnp.float32, -1.0, 1.0)
    shared_rho = jax.random.uniform(rho_key, (EMBED,), jnp.float32, 0.2, 0.9)
    own_noise = jax.random.truncated_normal(noise_key, -4.0, 4.0, (PAIRS, EMBED), jnp.float32)
    common = common_part(factors, labels, weights) * mixing
    inner = shared_rho * base_noise + jnp.sqrt(1.0 - shared_rho * shared_rho) * own_noise + common
    value = row_scale * column_scale * inner + offsets * column_scale
    return jnp.clip(value, -300.0, 300.0).astype(jnp.bfloat16)


def setup_inputs(seed: int = 0) -> dict:
    keys = jax.random.split(jax.random.key(seed), 3)
    embed_a = draw_embed_a(jax.random.fold_in(keys[2], 71), 0)
    embed_b = draw_embed_b(jax.random.fold_in(keys[2], 71), 0)
    return dict(embed_a=embed_a, embed_b=embed_b)


off_weight = 0.0051
epsilon = 1e-05

def normalize(embed):
    value = embed.astype(jnp.float32)
    mean_value = lax.optimization_barrier(jnp.mean(value, 0))
    centred = value - mean_value
    var_value = lax.optimization_barrier(jnp.mean(centred * centred, 0))
    scale_value = lax.rsqrt(var_value + epsilon)
    return ((centred * scale_value).astype(jnp.bfloat16), scale_value)

def norm_back(back_rows, normed, scale_value):
    plain = normed.astype(jnp.float32)
    first_mean = lax.optimization_barrier(jnp.mean(back_rows, 0))
    second_mean = lax.optimization_barrier(jnp.mean(back_rows * plain, 0))
    return ((back_rows - first_mean - plain * second_mean) * scale_value).astype(jnp.bfloat16)

def reference(embed_a, embed_b):
    batch_total, full_width = embed_a.shape
    norm_a, scale_a = normalize(embed_a)
    norm_b, scale_b = normalize(embed_b)
    cross_corr = jnp.dot(norm_a.T, norm_b, preferred_element_type=jnp.float32) / batch_total
    row_ids = lax.broadcasted_iota(jnp.int32, (full_width, full_width), 0)
    col_ids = lax.broadcasted_iota(jnp.int32, (full_width, full_width), 1)
    diagonal = row_ids == col_ids
    loss_total = jnp.sum(jnp.where(diagonal, (1.0 - cross_corr) ** 2, off_weight * cross_corr * cross_corr))
    slope_rows = jnp.where(diagonal, 2.0 * (cross_corr - 1.0), 2.0 * off_weight * cross_corr).astype(jnp.bfloat16)
    back_a = jnp.dot(norm_b, slope_rows.T, preferred_element_type=jnp.float32)
    back_b = jnp.dot(norm_a, slope_rows, preferred_element_type=jnp.float32)
    grad_a = norm_back(back_a, norm_a, scale_a)
    grad_b = norm_back(back_b, norm_b, scale_b)
    return (grad_a, grad_b, loss_total / full_width)
```

```python
import jax
import jax.numpy as jnp
from jax import lax
from jax.sharding import Mesh, PartitionSpec as P

off_weight = 0.0051
epsilon = 1e-05

PLANE = ("y", "xh", "co")
BATCH = ("xl", "z")
f32 = jnp.float32
bf16 = jnp.bfloat16


def swap(value, axis):
    return lax.ppermute(value, axis, [(0, 1), (1, 0)])


def butterfly(value, axis):
    size = lax.axis_size(axis)
    step = 1
    while step < size:
        value = value + lax.ppermute(value, axis, [(i, i ^ step) for i in range(size)])
        step *= 2
    return value


def transpose_blocks(value):
    pairs = [(g * 4 + f, f * 4 + g) for g in range(4) for f in range(4)]
    return lax.ppermute(value, PLANE, pairs)


def on_device(embed_a, embed_b):
    rows, width = embed_a.shape
    y, xl, z = lax.axis_index("y"), lax.axis_index("xl"), lax.axis_index("z")
    xh, co = lax.axis_index("xh"), lax.axis_index("co")
    parts = 16
    group_rows = rows * 4
    total = group_rows * parts
    full_width = width * 4

    with jax.named_scope("gather"):
        block_a = lax.all_gather(embed_a, "y", axis=0, tiled=True)
        mine = transpose_blocks(embed_b)
        theirs = swap(mine, "xh")
        pair = jnp.concatenate(
            [jnp.where(xh == 0, mine, theirs), jnp.where(xh == 0, theirs, mine)], 0
        )
        other = swap(pair, "co")
        even = jnp.where(co == 0, pair, other)
        odd = jnp.where(co == 0, other, pair)
        block_b = jnp.concatenate([even[:rows], odd[:rows], even[rows:], odd[rows:]], 0)

    with jax.named_scope("local_stats"):
        value_a = block_a.astype(f32)
        value_b = block_b.astype(f32)
        local_a = jnp.sum(value_a, 0) / group_rows
        local_b = jnp.sum(value_b, 0) / group_rows
        cent_a = value_a - local_a
        cent_b = value_b - local_b
        stats = jnp.stack(
            [
                local_a,
                jnp.sum(cent_a * cent_a, 0),
                local_b,
                jnp.sum(cent_b * cent_b, 0),
                jnp.sum(cent_a * cent_b, 0),
            ]
        )

    with jax.named_scope("corr"):
        product = lax.dot_general(
            cent_a.astype(bf16),
            cent_b.astype(bf16),
            (((0,), (0,)), ((), ())),
            preferred_element_type=f32,
        ).astype(bf16)
        summed = lax.psum_scatter(product, "z", scatter_dimension=0, tiled=True)
        half = summed.shape[0] // 2
        low, high = summed[:half], summed[half:]
        received = swap(jnp.where(xl == 0, high, low), "xl")
        piece = jnp.where(xl == 0, low, high).astype(f32) + received.astype(f32)

    with jax.named_scope("global_stats"):
        every = lax.all_gather(stats, BATCH)
        mean_a = jnp.sum(every[:, 0], 0) / parts
        mean_b = jnp.sum(every[:, 2], 0) / parts
        shift_a = every[:, 0] - mean_a
        shift_b = every[:, 2] - mean_b
        var_a = (jnp.sum(every[:, 1], 0) + group_rows * jnp.sum(shift_a * shift_a, 0)) / total
        var_b = (jnp.sum(every[:, 3], 0) + group_rows * jnp.sum(shift_b * shift_b, 0)) / total
        scale_a = lax.rsqrt(var_a + epsilon)
        scale_b = lax.rsqrt(var_b + epsilon)
        diag_corr = (
            (jnp.sum(every[:, 4], 0) + group_rows * jnp.sum(shift_a * shift_b, 0))
            / total
            * scale_a
            * scale_b
        )

    with jax.named_scope("norm"):
        norm_a = ((value_a - mean_a) * scale_a).astype(bf16)
        norm_b = ((value_b - mean_b) * scale_b).astype(bf16)
        plain_a = norm_a.astype(f32)
        plain_b = norm_b.astype(f32)
        norm_sums = jnp.stack([jnp.sum(plain_a, 0), jnp.sum(plain_b, 0)])

    with jax.named_scope("slope"):
        diagonal_block = y == xh * 2 + co
        first_row = z * (2 * half) + xl * half
        row_shift = lax.dynamic_slice_in_dim(shift_a, first_row, half, 1)
        row_scale = lax.dynamic_slice_in_dim(scale_a, first_row, half, 0)
        between = lax.dot_general(
            row_shift,
            shift_b,
            (((0,), (0,)), ((), ())),
            precision=lax.Precision.HIGHEST,
            preferred_element_type=f32,
        )
        corr = (piece + group_rows * between) * (row_scale[:, None] * (scale_b / total))
        row_ids = first_row + lax.broadcasted_iota(jnp.int32, corr.shape, 0)
        col_ids = lax.broadcasted_iota(jnp.int32, corr.shape, 1)
        diagonal = jnp.logical_and(row_ids == col_ids, diagonal_block)
        diag_slope = (2.0 * (diag_corr - 1.0)).astype(bf16)
        slope_piece = jnp.where(
            diagonal, diag_slope[None, :], (2.0 * off_weight * corr).astype(bf16)
        )
        loss_piece = jnp.sum(
            jnp.where(diagonal, (1.0 - diag_corr) ** 2, off_weight * corr * corr)
        )
        slope_other = swap(slope_piece, "xl")
        slope_pair = jnp.concatenate(
            [
                jnp.where(xl == 0, slope_piece, slope_other),
                jnp.where(xl == 0, slope_other, slope_piece),
            ],
            0,
        )
        slope = lax.all_gather(slope_pair, "z", axis=0, tiled=True)

    with jax.named_scope("small_sums"):
        small = jnp.concatenate([norm_sums, jnp.full((1, width), loss_piece)], 0)
        small = butterfly(butterfly(small, "xl"), "z")
        loss_total = small[2:3, :128]
        loss_total = butterfly(butterfly(butterfly(loss_total, "co"), "xh"), "y")
        loss_mean = loss_total[0, 0] / full_width
        centre_a = small[0:1] / total
        centre_b = small[1:2] / total

    with jax.named_scope("back"):
        wide = slope.astype(f32)
        eye = jnp.logical_and(
            lax.broadcasted_iota(jnp.int32, slope.shape, 0)
            == lax.broadcasted_iota(jnp.int32, slope.shape, 1),
            diagonal_block,
        )
        squares = jnp.where(eye, 0.0, wide * wide) / (2.0 * off_weight)
        diag_term = jnp.where(diagonal_block, diag_slope.astype(f32) * diag_corr, 0.0)
        two_a = jnp.sum(squares, 1) + diag_term
        two_b = jnp.sum(squares, 0) + diag_term
        one_a = jnp.sum(wide * centre_b, 1)
        one_b = jnp.sum(wide * centre_a.reshape(width, 1), 0)
        back_a = lax.dot_general(
            norm_b, slope, (((1,), (1,)), ((), ())), preferred_element_type=f32
        )
        part_a = ((back_a - one_a - plain_a * two_a) * scale_a).astype(bf16)
        back_b = jnp.dot(norm_a, slope, preferred_element_type=f32)
        part_b = ((back_b - one_b - plain_b * two_b) * scale_b).astype(bf16)

    with jax.named_scope("reduce"):
        grad_a = lax.psum_scatter(part_a, "y", scatter_dimension=0, tiled=True)
        quarters = part_b.reshape(2, 2, rows, width)
        even, odd = quarters[:, 0], quarters[:, 1]
        received = swap(jnp.where(co == 0, odd, even), "co")
        pair = jnp.where(co == 0, even, odd).astype(f32) + received.astype(f32)
        received = swap(jnp.where(xh == 0, pair[1], pair[0]).astype(bf16), "xh")
        mine = jnp.where(xh == 0, pair[0], pair[1]) + received.astype(f32)
        grad_b = transpose_blocks(mine.astype(bf16))
    return (grad_a, grad_b, loss_mean)


def solution(mesh):
    fine = Mesh(mesh.devices.reshape(4, 2, 8, 2, 2), ("y", "xl", "z", "xh", "co"))
    placed = P(("y", "xl", "z"), ("xh", "co"))
    return jax.shard_map(
        on_device,
        mesh=fine,
        in_specs=(placed, placed),
        out_specs=(placed, placed, P()),
        check_vma=False,
    )
```

```python
import jax
import jax.numpy as jnp
from jax import lax
from jax.sharding import Mesh, PartitionSpec as P

off_weight = 0.0051
epsilon = 1e-05

PLANE = ("y", "xh", "co")
BATCH = ("xl", "z")
f32 = jnp.float32
bf16 = jnp.bfloat16


def swap(value, axis):
    return lax.ppermute(value, axis, [(0, 1), (1, 0)])


def butterfly(value, axis):
    size = lax.axis_size(axis)
    step = 1
    while step < size:
        value = value + lax.ppermute(value, axis, [(i, i ^ step) for i in range(size)])
        step *= 2
    return value


def transpose_blocks(value):
    pairs = [(g * 4 + f, f * 4 + g) for g in range(4) for f in range(4)]
    return lax.ppermute(value, PLANE, pairs)


def on_device(embed_a, embed_b):
    rows, width = embed_a.shape
    y, xl, z = lax.axis_index("y"), lax.axis_index("xl"), lax.axis_index("z")
    xh, co = lax.axis_index("xh"), lax.axis_index("co")
    parts = 16
    group_rows = rows * 4
    total = group_rows * parts
    full_width = width * 4

    with jax.named_scope("gather"):
        block_a = lax.all_gather(embed_a, "y", axis=0, tiled=True)
        mine = transpose_blocks(embed_b)
        theirs = swap(mine, "xh")
        pair = jnp.concatenate(
            [jnp.where(xh == 0, mine, theirs), jnp.where(xh == 0, theirs, mine)], 0
        )
        other = swap(pair, "co")
        even = jnp.where(co == 0, pair, other)
        odd = jnp.where(co == 0, other, pair)
        block_b = lax.optimization_barrier(
            jnp.concatenate([even[:rows], odd[:rows], even[rows:], odd[rows:]], 0)
        )

    with jax.named_scope("local_stats"):
        value_a = block_a.astype(f32)
        value_b = block_b.astype(f32)
        local_a = jnp.sum(value_a, 0) / group_rows
        local_b = jnp.sum(value_b, 0) / group_rows
        cent_a = value_a - local_a
        cent_b = value_b - local_b
        stats = jnp.stack(
            [
                local_a,
                jnp.sum(cent_a * cent_a, 0),
                local_b,
                jnp.sum(cent_b * cent_b, 0),
                jnp.sum(cent_a * cent_b, 0),
            ]
        )

    with jax.named_scope("corr"):
        product = lax.dot_general(
            cent_a.astype(bf16),
            cent_b.astype(bf16),
            (((0,), (0,)), ((), ())),
            preferred_element_type=f32,
        ).astype(bf16)
        summed = lax.psum_scatter(product, "z", scatter_dimension=0, tiled=True)
        piece = summed.astype(f32) + swap(summed, "xl").astype(f32)

    with jax.named_scope("global_stats"):
        every = lax.all_to_all(
            jnp.broadcast_to(stats, (parts,) + stats.shape), BATCH, 0, 0, tiled=True
        )
        mean_a = jnp.sum(every[:, 0], 0) / parts
        mean_b = jnp.sum(every[:, 2], 0) / parts
        shift_a = every[:, 0] - mean_a
        shift_b = every[:, 2] - mean_b
        var_a = (jnp.sum(every[:, 1], 0) + group_rows * jnp.sum(shift_a * shift_a, 0)) / total
        var_b = (jnp.sum(every[:, 3], 0) + group_rows * jnp.sum(shift_b * shift_b, 0)) / total
        scale_a = lax.rsqrt(var_a + epsilon)
        scale_b = lax.rsqrt(var_b + epsilon)
        diag_corr = (
            (jnp.sum(every[:, 4], 0) + group_rows * jnp.sum(shift_a * shift_b, 0))
            / total
            * scale_a
            * scale_b
        )

    with jax.named_scope("norm"):
        norm_a, norm_b = lax.optimization_barrier(
            (
                ((value_a - mean_a) * scale_a).astype(bf16),
                ((value_b - mean_b) * scale_b).astype(bf16),
            )
        )
        plain_a = norm_a.astype(f32)
        plain_b = norm_b.astype(f32)
        norm_sums = jnp.stack([jnp.sum(plain_a, 0), jnp.sum(plain_b, 0)])

    with jax.named_scope("slope"):
        diagonal_block = y == xh * 2 + co
        height = piece.shape[0]
        first_row = z * height
        row_shift = lax.dynamic_slice_in_dim(shift_a, first_row, height, 1)
        row_scale = lax.dynamic_slice_in_dim(scale_a, first_row, height, 0)
        between = lax.dot_general(
            row_shift,
            shift_b,
            (((0,), (0,)), ((), ())),
            precision=lax.Precision.HIGHEST,
            preferred_element_type=f32,
        )
        corr = (piece + group_rows * between) * (row_scale[:, None] * (scale_b / total))
        row_ids = first_row + lax.broadcasted_iota(jnp.int32, corr.shape, 0)
        col_ids = lax.broadcasted_iota(jnp.int32, corr.shape, 1)
        diagonal = jnp.logical_and(row_ids == col_ids, diagonal_block)
        diag_slope = (2.0 * (diag_corr - 1.0)).astype(bf16)
        slope_piece = jnp.where(
            diagonal, diag_slope[None, :], (2.0 * off_weight * corr).astype(bf16)
        )
        slope = lax.all_gather(slope_piece, "z", axis=0, tiled=True)

    with jax.named_scope("small_sums"):
        exact = jnp.where(diagonal, diag_corr[None, :], corr)
        weighed = 0.5 * (slope_piece.astype(f32) * exact)
        loss_piece = 0.5 * jnp.sum(
            jnp.where(diagonal, (1.0 - exact) ** 2, off_weight * exact * exact)
        )
        placed = lax.dynamic_update_slice_in_dim(
            jnp.zeros((width,), f32), jnp.sum(weighed, 1), first_row, 0
        )
        small = jnp.concatenate(
            [
                norm_sums,
                placed[None],
                jnp.sum(weighed, 0)[None],
                jnp.full((1, width), loss_piece),
            ],
            0,
        )
        small = butterfly(butterfly(small, "xl"), "z")
        loss_total = small[4:5, :128]
        loss_total = butterfly(butterfly(butterfly(loss_total, "co"), "xh"), "y")
        slope, small, loss_total = lax.optimization_barrier((slope, small, loss_total))
        loss_mean = loss_total[0, 0] / full_width
        centre_a = small[0] / total
        centre_b = small[1] / total
        two_a = small[2]
        two_b = small[3]

    with jax.named_scope("back"):
        wide = slope.astype(f32)
        one_a = jnp.sum(wide * centre_b, 1)
        one_b = jnp.sum(wide * centre_a.reshape(width, 1), 0)
        back_b = jnp.dot(norm_a, slope, preferred_element_type=f32)
        part_b = ((back_b - one_b - plain_b * two_b) * scale_b).astype(bf16)
        part_b, norm_b, slope = lax.optimization_barrier((part_b, norm_b, slope))
        back_a = lax.dot_general(
            norm_b, slope, (((1,), (1,)), ((), ())), preferred_element_type=f32
        )
        part_a = ((back_a - one_a - plain_a * two_a) * scale_a).astype(bf16)

    with jax.named_scope("reduce"):
        grad_a = lax.psum_scatter(part_a, "y", scatter_dimension=0, tiled=True)
        quarters = part_b.reshape(2, 2, rows, width)
        even, odd = quarters[:, 0], quarters[:, 1]
        received = swap(jnp.where(co == 0, odd, even), "co")
        pair = jnp.where(co == 0, even, odd).astype(f32) + received.astype(f32)
        received = swap(jnp.where(xh == 0, pair[1], pair[0]).astype(bf16), "xh")
        mine = jnp.where(xh == 0, pair[0], pair[1]) + received.astype(f32)
        grad_b = transpose_blocks(mine.astype(bf16))
    return (grad_a, grad_b, loss_mean)


def solution(mesh):
    fine = Mesh(mesh.devices.reshape(4, 2, 8, 2, 2), ("y", "xl", "z", "xh", "co"))
    placed = P(("y", "xl", "z"), ("xh", "co"))
    return jax.shard_map(
        on_device,
        mesh=fine,
        in_specs=(placed, placed),
        out_specs=(placed, placed, P()),
        check_vma=False,
    )
```

```python
import functools

import jax
import jax.numpy as jnp
from jax import lax
from jax.experimental import pallas as pl
from jax.experimental.pallas import tpu as pltpu
from jax.sharding import Mesh, PartitionSpec as P

off_weight = 0.0051
epsilon = 1e-05

PLANE = ("y", "xh", "co")
BATCH = ("xl", "z")
f32 = jnp.float32
bf16 = jnp.bfloat16


def swap(value, axis):
    return lax.ppermute(value, axis, [(0, 1), (1, 0)])


def butterfly(value, axis):
    size = lax.axis_size(axis)
    step = 1
    while step < size:
        value = value + lax.ppermute(value, axis, [(i, i ^ step) for i in range(size)])
        step *= 2
    return value


def transpose_blocks(value):
    pairs = [(g * 4 + f, f * 4 + g) for g in range(4) for f in range(4)]
    return lax.ppermute(value, PLANE, pairs)


PARAMS = pltpu.CompilerParams(vmem_limit_bytes=48 * 1024 * 1024)


def corr_kernel(order_ref, a_ref, b0_ref, b1_ref, b2_ref, b3_ref, out_ref, mean_ref, ca_ref, cb_ref):
    rows = b0_ref.shape[0]
    count = 4 * rows
    width = out_ref.shape[1]
    pieces = (b0_ref, b1_ref, b2_ref, b3_ref)
    ones = jnp.ones((16, rows), bf16)
    sum_a = jnp.zeros((16, width), f32)
    sum_b = jnp.zeros((16, width), f32)
    for place, piece in enumerate(pieces):
        sum_a += jnp.dot(ones, a_ref[place], preferred_element_type=f32)
        sum_b += jnp.dot(ones, piece[...], preferred_element_type=f32)
    mean_a = sum_a[:1] / count
    mean_b = sum_b[:1] / count
    mean_ref[0:1] = mean_a
    mean_ref[1:2] = mean_b
    for place, piece in enumerate(pieces):
        part = slice(place * rows, (place + 1) * rows)
        ca_ref[part] = (a_ref[order_ref[place]].astype(f32) - mean_a).astype(bf16)
        cb_ref[part] = (piece[...].astype(f32) - mean_b).astype(bf16)
    chunk = min(256, width)
    for start in range(0, width, chunk):
        part = slice(start, start + chunk)
        out_ref[part] = lax.dot_general(
            ca_ref[:, part], cb_ref[...], (((0,), (0,)), ((), ())), preferred_element_type=f32
        ).astype(bf16)


def corr_call(order, block_a, pieces):
    rows, width = pieces[0].shape
    whole = pl.BlockSpec(memory_space=pltpu.VMEM)
    return pl.pallas_call(
        corr_kernel,
        out_shape=(
            jax.ShapeDtypeStruct((width, width), bf16),
            jax.ShapeDtypeStruct((2, width), f32),
        ),
        in_specs=[pl.BlockSpec(memory_space=pltpu.SMEM)] + [whole] * 5,
        out_specs=(whole, whole),
        scratch_shapes=[pltpu.VMEM((4 * rows, width), bf16)] * 2,
        compiler_params=PARAMS,
        cost_estimate=pl.CostEstimate(
            flops=8 * rows * width * width, bytes_accessed=24 * rows * width, transcendentals=0
        ),
        name="corr",
    )(order, block_a.reshape(4, rows, width), *pieces)


def back_rows(dims, left_ref, slope_ref, plain_ref, centre_ref, vec_ref):
    slope = slope_ref[...]
    back = lax.dot_general(left_ref[...], slope, dims, preferred_element_type=f32)
    one = lax.dot_general(centre_ref[...], slope, dims, preferred_element_type=f32)
    one = one[0:1] + one[1:2]
    return (back - one - plain_ref[...].astype(f32) * vec_ref[0:1]) * vec_ref[1:2]


AS_IS = (((1,), (0,)), ((), ()))
TURNED = (((1,), (1,)), ((), ()))


def back_kernel(dims, order_ref, left_ref, slope_ref, plain_ref, centre_ref, vec_ref, out_ref):
    out_ref[...] = back_rows(dims, left_ref, slope_ref, plain_ref, centre_ref, vec_ref).astype(bf16)


def keep_kernel(
    dims, order_ref, left_ref, slope_ref, plain_ref, centre_ref, vec_ref, got_ref, send_ref, mine_ref
):
    value = back_rows(dims, left_ref, slope_ref, plain_ref, centre_ref, vec_ref)
    value = value + got_ref[...].astype(f32)
    step = pl.program_id(0)

    @pl.when(step == 0)
    def _():
        send_ref[...] = value.astype(bf16)

    @pl.when(step == 1)
    def _():
        mine_ref[...] = value


def back_call(dims, order, steps, rows, left, slope, plain, centre, vec, got=None):
    width = slope.shape[0]
    picked = pl.BlockSpec((rows, width), lambda i, order: (order[i], 0))
    fixed = lambda height: pl.BlockSpec((height, width), lambda i, order: (0, 0))
    in_specs = [picked, fixed(width), picked, fixed(16), fixed(2)]
    args = [left, slope, plain, centre, vec]
    if got is None:
        kernel = back_kernel
        out_shape = jax.ShapeDtypeStruct((steps * rows, width), bf16)
        out_specs = pl.BlockSpec((rows, width), lambda i, order: (i, 0))
    else:
        kernel = keep_kernel
        in_specs.append(pl.BlockSpec((rows, width), lambda i, order: (order[2 + i], 0)))
        args.append(got)
        out_shape = (
            jax.ShapeDtypeStruct((rows, width), bf16),
            jax.ShapeDtypeStruct((rows, width), f32),
        )
        out_specs = (fixed(rows), fixed(rows))
    return pl.pallas_call(
        functools.partial(kernel, dims),
        out_shape=out_shape,
        grid_spec=pltpu.PrefetchScalarGridSpec(
            num_scalar_prefetch=1, grid=(steps,), in_specs=in_specs, out_specs=out_specs
        ),
        compiler_params=PARAMS,
        cost_estimate=pl.CostEstimate(
            flops=2 * steps * rows * width * width,
            bytes_accessed=6 * steps * rows * width + 2 * width * width,
            transcendentals=0,
        ),
        name="back",
    )(order, *args)


def split_rows(row):
    high = row.astype(bf16)
    low = (row - high.astype(f32)).astype(bf16)
    return jnp.concatenate([high[None], low[None], jnp.zeros((14, row.shape[0]), bf16)], 0)


def on_device(embed_a, embed_b):
    rows, width = embed_a.shape
    y, xl, z = lax.axis_index("y"), lax.axis_index("xl"), lax.axis_index("z")
    xh, co = lax.axis_index("xh"), lax.axis_index("co")
    parts = 16
    group_rows = rows * 4
    total = group_rows * parts
    full_width = width * 4

    with jax.named_scope("gather"):
        block_a = lax.all_gather(embed_a, "y", axis=0, tiled=True)
        mine = transpose_blocks(embed_b)
        theirs = swap(mine, "xh")
        mine_other = swap(mine, "co")
        theirs, block_a = lax.optimization_barrier((theirs, block_a))
        theirs_other = swap(theirs, "co")
        pieces = (mine, theirs, mine_other, theirs_other)
        order = jnp.stack(
            [2 * xh + co, 2 * (1 - xh) + co, 2 * xh + 1 - co, 2 * (1 - xh) + 1 - co]
        ).astype(jnp.int32)

    with jax.named_scope("corr"):
        product, local = corr_call(order, block_a, pieces)
        summed = lax.psum_scatter(product, "z", scatter_dimension=0, tiled=True)
        piece = summed.astype(f32) + swap(summed, "xl").astype(f32)

    with jax.named_scope("local_stats"):
        pieces, local = lax.optimization_barrier((pieces, local))
        low = jnp.where(co == 0, jnp.stack(pieces[:2]), jnp.stack(pieces[2:]))
        high = jnp.where(co == 0, jnp.stack(pieces[2:]), jnp.stack(pieces[:2]))
        even = jnp.where(xh == 0, low, low[::-1])
        odd = jnp.where(xh == 0, high, high[::-1])
        block_b = jnp.stack([even[0], odd[0], even[1], odd[1]]).reshape(group_rows, width)
        block_b = lax.optimization_barrier(block_b)
        value_a = block_a.astype(f32)
        value_b = block_b.astype(f32)
        cent_a = value_a - local[0]
        cent_b = value_b - local[1]
        stats = jnp.stack(
            [
                local[0],
                jnp.sum(cent_a * cent_a, 0),
                local[1],
                jnp.sum(cent_b * cent_b, 0),
                jnp.sum(cent_a * cent_b, 0),
            ]
        )

    with jax.named_scope("global_stats"):
        every = lax.all_gather(stats, BATCH)
        mean_a = jnp.sum(every[:, 0], 0) / parts
        mean_b = jnp.sum(every[:, 2], 0) / parts
        shift_a = every[:, 0] - mean_a
        shift_b = every[:, 2] - mean_b
        var_a = (jnp.sum(every[:, 1], 0) + group_rows * jnp.sum(shift_a * shift_a, 0)) / total
        var_b = (jnp.sum(every[:, 3], 0) + group_rows * jnp.sum(shift_b * shift_b, 0)) / total
        scale_a = lax.rsqrt(var_a + epsilon)
        scale_b = lax.rsqrt(var_b + epsilon)
        diag_corr = (
            (jnp.sum(every[:, 4], 0) + group_rows * jnp.sum(shift_a * shift_b, 0))
            / total
            * scale_a
            * scale_b
        )

    with jax.named_scope("norm"):
        norm_a, norm_b = lax.optimization_barrier(
            (
                ((value_a - mean_a) * scale_a).astype(bf16),
                ((value_b - mean_b) * scale_b).astype(bf16),
            )
        )
        plain_a = norm_a.astype(f32)
        plain_b = norm_b.astype(f32)
        norm_sums = jnp.stack([jnp.sum(plain_a, 0), jnp.sum(plain_b, 0)])

    with jax.named_scope("slope"):
        diagonal_block = y == xh * 2 + co
        height = piece.shape[0]
        first_row = z * height
        row_shift = lax.dynamic_slice_in_dim(shift_a, first_row, height, 1)
        row_scale = lax.dynamic_slice_in_dim(scale_a, first_row, height, 0)
        between = lax.dot_general(
            row_shift,
            shift_b,
            (((0,), (0,)), ((), ())),
            precision=lax.Precision.HIGHEST,
            preferred_element_type=f32,
        )
        corr = (piece + group_rows * between) * (row_scale[:, None] * (scale_b / total))
        row_ids = first_row + lax.broadcasted_iota(jnp.int32, corr.shape, 0)
        col_ids = lax.broadcasted_iota(jnp.int32, corr.shape, 1)
        diagonal = jnp.logical_and(row_ids == col_ids, diagonal_block)
        diag_slope = (2.0 * (diag_corr - 1.0)).astype(bf16)
        slope_piece = jnp.where(
            diagonal, diag_slope[None, :], (2.0 * off_weight * corr).astype(bf16)
        )
        slope = lax.all_gather(slope_piece, "z", axis=0, tiled=True)

    with jax.named_scope("small_sums"):
        exact = jnp.where(diagonal, diag_corr[None, :], corr)
        weighed = 0.5 * (slope_piece.astype(f32) * exact)
        loss_piece = 0.5 * jnp.sum(
            jnp.where(diagonal, (1.0 - exact) ** 2, off_weight * exact * exact)
        )
        placed = lax.dynamic_update_slice_in_dim(
            jnp.zeros((width,), f32), jnp.sum(weighed, 1), first_row, 0
        )
        small = jnp.concatenate(
            [
                norm_sums,
                placed[None],
                jnp.sum(weighed, 0)[None],
                jnp.full((1, width), loss_piece),
            ],
            0,
        )
        small = butterfly(butterfly(small, "xl"), "z")
        loss_total = small[4:5, :128]
        loss_total = butterfly(butterfly(butterfly(loss_total, "co"), "xh"), "y")
        slope, small, loss_total = lax.optimization_barrier((slope, small, loss_total))
        loss_mean = loss_total[0, 0] / full_width
        centre_a = small[0] / total
        centre_b = small[1] / total
        two_a = small[2]
        two_b = small[3]

        vec_a = jnp.stack([two_a, scale_a])
        vec_b = jnp.stack([two_b, scale_b])
        centre_a = split_rows(centre_a)
        centre_b = split_rows(centre_b)

    with jax.named_scope("back"):
        order = jnp.stack([1 - co, 3 - co]).astype(jnp.int32)
        sent = back_call(AS_IS, order, 2, rows, norm_a, slope, norm_b, centre_a, vec_b)
        received = swap(sent, "co")
        slope, sent = lax.optimization_barrier((slope, sent))
        order = jnp.arange(4, dtype=jnp.int32)
        part_a = back_call(TURNED, order, 4, rows, norm_b, slope, norm_a, centre_b, vec_a)
        grad_a = lax.psum_scatter(part_a, "y", scatter_dimension=0, tiled=True)
        order = jnp.stack([2 * (1 - xh) + co, 2 * xh + co, 1 - xh, xh]).astype(jnp.int32)
        sent, mine = back_call(
            AS_IS, order, 2, rows, norm_a, slope, norm_b, centre_a, vec_b, received
        )
        received = swap(sent, "xh")
        grad_b = transpose_blocks((mine + received.astype(f32)).astype(bf16))
    return (grad_a, grad_b, loss_mean)


def solution(mesh):
    fine = Mesh(mesh.devices.reshape(4, 2, 8, 2, 2), ("y", "xl", "z", "xh", "co"))
    placed = P(("y", "xl", "z"), ("xh", "co"))
    return jax.shard_map(
        on_device,
        mesh=fine,
        in_specs=(placed, placed),
        out_specs=(placed, placed, P()),
        check_vma=False,
    )
```
